32 devices in a mesh: group: 2 (over y), seq: 16 (over z, x, core).
Axes of the slice: x: 2, y: 2, z: 4, core: 2. Of those that a mesh axis runs over, the one named last changes fastest.
Arguments:
- prompt_queries: bfloat16 [2048, 4096], P(('group', 'seq')), parts along dimension 0, may hold values from -80 to 80
- prompt_keys: bfloat16 [2048, 512], P(('group', 'seq')), parts along dimension 0, may hold values from -4 to 4
- prompt_values: bfloat16 [2048, 512], P(('group', 'seq')), parts along dimension 0, may hold values from -5 to 5
- prompt_positions: int32 [2048], P(('group', 'seq')), parts along dimension 0, may hold values from 0 to 1023, as said below
- step_queries: bfloat16 [32, 2, 4096], P(('group', 'seq')), parts along dimension 0, may hold values from -80 to 80
- step_keys: bfloat16 [32, 2, 512], P(('group', 'seq')), parts along dimension 0, may hold values from -5 to 5
- step_values: bfloat16 [32, 2, 512], P(('group', 'seq')), parts along dimension 0, may hold values from -5 to 5
- pool_keys: bfloat16 [1024, 128, 512], P(('group', 'seq')), parts along dimension 0, may hold values from -4 to 4
- pool_values: bfloat16 [1024, 128, 512], P(('group', 'seq')), parts along dimension 0, may hold values from -5 to 5
- page_owner: int32 [1024, 1], P(('group', 'seq')), parts along dimension 0, may hold values from 0 to 15
- page_fill: int32 [1024], P(('group', 'seq')), parts along dimension 0, may hold values from 1 to 128
Outputs:
- prefill_out: bfloat16 [2048, 4096], P(('group', 'seq')), parts along dimension 0
- decode_out: bfloat16 [32, 2, 4096], P(('group', 'seq')), parts along dimension 0
The draws below stay inside these ranges and needn't reach their ends.
There are 2 independent parts, one for each index of `group`. The reference program is written for one: setup_inputs(seed, part) draws one part's arguments, and reference() takes and returns one part's arrays. A program takes and returns all parts, laid end to end along the dimension named above; each array names one. Nothing has to cross between parts.
Inputs may be any that keep to these rules, and one draw needn't show every extreme that they name: `prompt_positions`: each device's 64 rows are two runs of consecutive positions, each of half of 64 rows and starting at a multiple of that half; every position of 0 to 1023 appears once. `page_owner`: every decode sequence owns at least one page.
All inputs are finite; a program needn't handle non-finite values.
Results may differ from the reference program's by a relative error of at most 0.009.
Values may be sent and summed in bfloat16 or wider, within the bound.
A program may use at most 192 MiB of HBM per device.

```python
import functools
import math
import jax
import jax.numpy as jnp
from jax import lax

QH = 32
KVH = 4
HD = 128
TOK_DEV = 64
PAGE = 128
STEPS = 2
TOKENS = 1024
PAGES = 512
B = 16


def prompt_key_base(key):
    return jnp.clip(jax.random.normal(key, (TOKENS, KVH * HD), jnp.float32), -4.0, 4.0)


def step_key_base(key):
    return jnp.clip(jax.random.normal(key, (B, STEPS, KVH * HD), jnp.float32), -4.0, 4.0)


def draw_prompt_keys(key, part):
    base = prompt_key_base(key)
    return base.astype(jnp.bfloat16)


def draw_prompt_queries(key, part):
    key = jax.random.fold_in(key, 2)
    queries = 2.5 * jnp.clip(jax.random.normal(key, (TOKENS, QH * HD), jnp.float32), -4.0, 4.0)
    return queries.astype(jnp.bfloat16)


def draw_step_keys(key, part):
    base = step_key_base(key)
    return base.astype(jnp.bfloat16)


def draw_step_queries(key, part):
    key = jax.random.fold_in(key, 4)
    queries = 2.5 * jnp.clip(jax.random.normal(key, (B, STEPS, QH * HD), jnp.float32), -4.0, 4.0)
    return queries.astype(jnp.bfloat16)


def draw_prompt_positions(key, part):
    key = jax.random.fold_in(key, 5)
    device_count = TOKENS // TOK_DEV
    half_rows = TOK_DEV // 2
    order = jax.random.permutation(key, 2 * device_count).astype(jnp.int32)
    row_ids = jnp.arange(TOKENS, dtype=jnp.int32)
    device_ids = row_ids // TOK_DEV
    inside = row_ids % TOK_DEV
    slot_ids = 2 * device_ids + inside // half_rows
    return (jnp.take(order, slot_ids) * half_rows + inside % half_rows).astype(jnp.int32)


def place_ends(values, rng, least, high):
    shape = values.shape
    place = [jax.random.randint(jax.random.fold_in(rng, axis), (), 0, shape[axis]) for axis in range(len(shape))]
    values = values.at[tuple(place)].set(least)
    longest = shape.index(max(shape))
    place[longest] = (place[longest] + 1) % shape[longest]
    return values.at[tuple(place)].set(high)


def block_levels(rng, shape, cuts, smallest, top_value):
    level, own = 1.0, jax.random.fold_in(rng, 6)
    for position, blocks in cuts:
        steps = jnp.exp(jax.random.uniform(jax.random.fold_in(own, position), (blocks,), jnp.float32, smallest / len(cuts), top_value / len(cuts)))
        level = level * jnp.repeat(steps, shape[position] // blocks).reshape([-1 if axis == position else 1 for axis in range(len(shape))])
    return level


def choose_distinct(stream_key, rows, amount, top, lift):
    sequence = jax.random.permutation(jax.random.fold_in(stream_key, 1), amount)
    boost = sequence
    for power in range(3):
        boost = boost * boost // amount
    boost = boost * lift // amount
    tickets = jax.random.randint(jax.random.fold_in(stream_key, 2), (rows, amount), 0, 4096) + boost
    holders = jax.random.permutation(jax.random.fold_in(stream_key, 3), rows)[jnp.arange(amount) % rows]
    tickets = jnp.where(jnp.arange(rows)[:, None] == holders[None, :], 1 << 14, tickets)
    score = tickets * amount + jnp.arange(amount)
    return lax.top_k(score.astype(jnp.int32), top)[1].astype(jnp.int32)


def normal_values(stream_key, extent, spread, limit, shards=(), kind=jnp.bfloat16):
    values = jax.random.normal(stream_key, extent, jnp.float32) * spread
    if len(shards) > 0:
        values = block_levels(stream_key, extent, shards, -0.22, 0.18) * values
    return jnp.clip(values, min=-limit, max=limit).astype(kind)


def setup_inputs(seed: int = 0, part: int = 0) -> dict:
    streams_of = jax.random.split(jax.random.key(seed), 12)
    part_splits = jax.random.split(jax.random.fold_in(streams_of[11], part), 12)
    prompt_queries = draw_prompt_queries(jax.random.fold_in(jax.random.fold_in(streams_of[11], part), 71), part)
    prompt_keys = draw_prompt_keys(jax.random.fold_in(jax.random.fold_in(streams_of[11], part), 71), part)
    prompt_values = normal_values(part_splits[2], (TOKENS, KVH * HD), 1.0, 5.0, ((0, 16),))
    prompt_positions = draw_prompt_positions(jax.random.fold_in(jax.random.fold_in(streams_of[11], part), 71), part)
    step_queries = draw_step_queries(jax.random.fold_in(jax.random.fold_in(streams_of[11], part), 71), part)
    step_keys = draw_step_keys(jax.random.fold_in(jax.random.fold_in(streams_of[11], part), 71), part)
    step_values = normal_values(part_splits[6], (B, STEPS, KVH * HD), 1.0, 5.0, ((0, 16),))
    pool_keys = normal_values(part_splits[7], (PAGES, PAGE, KVH * HD), 1.0, 4.0, ((0, 16),))
    pool_values = normal_values(part_splits[8], (PAGES, PAGE, KVH * HD), 1.0, 5.0, ((0, 16),))
    page_owner = choose_distinct(part_splits[9], PAGES, B, 1, 1024)
    page_fill = place_ends(jax.random.randint(part_splits[10], (PAGES,), 1, PAGE + 1), jax.random.fold_in(part_splits[10], 1), 1, PAGE).astype(jnp.int32)
    return dict(prompt_queries=prompt_queries, prompt_keys=prompt_keys, prompt_values=prompt_values, prompt_positions=prompt_positions, step_queries=step_queries, step_keys=step_keys, step_values=step_values, pool_keys=pool_keys, pool_values=pool_values, page_owner=page_owner, page_fill=page_fill)


NEG_FILL = -1.0e30


def prefill_block(block_data, all_keys, all_values, key_positions):
    block_queries, block_positions = block_data
    row_count = block_queries.shape[0]
    group_size = QH // KVH
    query_heads = block_queries.astype(jnp.float32).reshape(row_count, KVH, group_size, HD)
    key_heads = all_keys.astype(jnp.float32).reshape(-1, KVH, HD)
    value_heads = all_values.reshape(-1, KVH, HD)
    scores = jnp.einsum("rkgd,skd->kgrs", query_heads, key_heads, precision=lax.Precision.HIGHEST) * (HD ** -0.5)
    allowed = key_positions[None, :] <= block_positions[:, None]
    scores = jnp.where(allowed[None, None], scores, NEG_FILL)
    row_max = jnp.max(scores, axis=-1, keepdims=True)
    weights = jnp.where(allowed[None, None], jnp.exp(scores - row_max), 0.0)
    denominator = jnp.sum(weights, axis=-1)
    rounded = weights.astype(jnp.bfloat16)
    numerator = jnp.einsum("kgrs,skd->rkgd", rounded, value_heads, preferred_element_type=jnp.float32)
    ratio = numerator / jnp.transpose(denominator, (2, 0, 1))[..., None]
    return ratio.reshape(row_count, QH * HD).astype(jnp.bfloat16)


def finish_steps(own_queries, own_keys, own_values, own_max, own_sum, own_total):
    seq_count = own_queries.shape[0]
    group_size = QH // KVH
    query_heads = own_queries.astype(jnp.float32).reshape(seq_count, STEPS, KVH, group_size, HD)
    key_heads = own_keys.astype(jnp.float32).reshape(seq_count, STEPS, KVH, HD)
    value_heads = own_values.astype(jnp.float32).reshape(seq_count, STEPS, KVH, HD)
    step_scores = jnp.einsum("bskgd,bjkd->bskgj", query_heads, key_heads, precision=lax.Precision.HIGHEST) * (HD ** -0.5)
    step_mask = jnp.arange(STEPS)[None, :] <= jnp.arange(STEPS)[:, None]
    mask_full = step_mask[None, :, None, None, :]
    step_scores = jnp.where(mask_full, step_scores, NEG_FILL)
    overall = jnp.maximum(own_max, jnp.max(step_scores, axis=-1))
    pool_scale = jnp.exp(own_max - overall)
    step_weights = jnp.where(mask_full, jnp.exp(step_scores - overall[..., None]), 0.0)
    numerator = pool_scale[..., None] * own_sum + jnp.einsum("bskgj,bjkd->bskgd", step_weights, value_heads, precision=lax.Precision.HIGHEST)
    denominator = pool_scale * own_total + jnp.sum(step_weights, axis=-1)
    result = numerator / denominator[..., None]
    return result.reshape(seq_count, STEPS, QH * HD).astype(jnp.bfloat16)


def reference(prompt_queries, prompt_keys, prompt_values, prompt_positions, step_queries, step_keys, step_values, pool_keys, pool_values, page_owner, page_fill):
    block_rows = math.gcd(TOKENS, 256)
    block_count = TOKENS // block_rows
    blocks = (prompt_queries.reshape(block_count, block_rows, QH * HD), prompt_positions.reshape(block_count, block_rows))
    one_block = functools.partial(prefill_block, all_keys=prompt_keys, all_values=prompt_values, key_positions=prompt_positions)
    prefill_out = lax.map(one_block, blocks).reshape(TOKENS, QH * HD)

    group_size = QH // KVH
    owner = page_owner[:, 0].astype(jnp.int32)
    page_count = pool_keys.shape[0]
    page_queries = jnp.take(step_queries, owner, axis=0).astype(jnp.float32).reshape(page_count, STEPS, KVH, group_size, HD)
    key_heads = pool_keys.astype(jnp.float32).reshape(page_count, PAGE, KVH, HD)
    value_heads = pool_values.astype(jnp.float32).reshape(page_count, PAGE, KVH, HD)
    scores = jnp.einsum("pskgd,pjkd->pskgj", page_queries, key_heads, precision=lax.Precision.HIGHEST) * (HD ** -0.5)
    valid = jnp.arange(PAGE)[None, :] < page_fill[:, None]
    valid_full = valid[:, None, None, None, :]
    scores = jnp.where(valid_full, scores, NEG_FILL)
    page_max = jnp.max(scores, axis=-1)
    pool_max = jax.ops.segment_max(page_max, owner, num_segments=B)
    page_top = jnp.take(pool_max, owner, axis=0)
    pool_weight = jnp.where(valid_full, jnp.exp(scores - page_top[..., None]), 0.0).astype(jnp.bfloat16)
    pool_weight = lax.optimization_barrier(pool_weight).astype(jnp.float32)
    page_sum = jnp.einsum("pskgj,pjkd->pskgd", pool_weight, value_heads, precision=lax.Precision.HIGHEST)
    page_total = jnp.sum(pool_weight, axis=-1)
    pool_sum = jax.ops.segment_sum(page_sum, owner, num_segments=B)
    pool_total = jax.ops.segment_sum(page_total, owner, num_segments=B)
    decode_out = finish_steps(step_queries, step_keys, step_values, pool_max, pool_sum, pool_total)
    return prefill_out, decode_out
```

```python
import functools
import jax
import jax.numpy as jnp
from jax import lax
from jax.experimental import pallas as pl
from jax.experimental.pallas import tpu as pltpu
from jax.sharding import PartitionSpec as P

QH = 32
KVH = 4
HD = 128
GROUP = QH // KVH
PAGE = 128
STEPS = 2
ROWS = STEPS * QH
HEAD_ROWS = STEPS * GROUP
MSG = ROWS + 16
SEQ_BLOCK = 16
NEG = -1e30
LOG2E = 1.4426950408889634
SCALE = HD ** (-0.5) * LOG2E
MESH = pl.DeviceIdType.MESH
NT = (((1,), (1,)), ((), ()))


def kernel(
    n,
    X,
    qmsg,
    row_pos,
    tok_owner,
    pq,
    own_k,
    own_v,
    step_k,
    step_v,
    pool_k_hbm,
    pool_v_hbm,
    out,
    dec,
    qall,
    kv,
    pool_k,
    pool_v,
    key_pos,
    psend,
    precv,
    stats,
    stats_in,
    pool_sem,
    q_send,
    q_sib,
    q_recv,
    p_send,
    p_recv,
    up_send,
    down_send,
    x_send,
    sib_send,
    kv_recv,
):
    Z = n // (2 * X)
    half = n // 2
    me = lax.axis_index("seq")
    c = lax.rem(me, 2)
    x = lax.rem(me // 2, X)
    z = me // (2 * X)
    sib = me + 1 - 2 * c
    tok = own_k.shape[0]
    keys = n * tok
    tokens = pool_k.shape[0]

    pool_copies = [
        pltpu.make_async_copy(pool_k_hbm, pool_k, pool_sem.at[0]),
        pltpu.make_async_copy(pool_v_hbm, pool_v, pool_sem.at[1]),
    ]
    barrier = pltpu.get_barrier_semaphore()

    def greet(i, carry):
        pl.semaphore_signal(
            barrier, inc=1, device_id={"seq": lax.rem(me + i, n)}, device_id_type=MESH
        )
        return carry

    lax.fori_loop(1, n, greet, 0)
    for copy in pool_copies:
        copy.start()
    qall[me] = qmsg[...]
    kv[me, :, : KVH * HD] = own_k[...]
    kv[me, :, KVH * HD :] = own_v[...]
    stats[...] = jnp.full_like(stats, NEG)
    stats_in[...] = jnp.full_like(stats_in, NEG)
    pl.semaphore_wait(barrier, n - 1)

    def remote(buf, b, peer, ss, rs):
        return pltpu.make_async_remote_copy(
            src_ref=buf.at[b],
            dst_ref=buf.at[b],
            send_sem=ss,
            recv_sem=rs.at[b],
            device_id={"seq": peer},
            device_id_type=MESH,
        )

    def q_copy(j):
        return remote(qall, me, lax.rem(me + 2 * j, n), q_send.at[j], q_recv)

    def q_fwd(j):
        b = lax.rem(me + 2 * j, n)
        return remote(qall, b, sib, q_sib.at[j], q_recv)

    def loop(lo, hi, body):
        def step(i, carry):
            body(i)
            return carry

        lax.fori_loop(lo, hi, step, 0)

    loop(1, half, lambda j: q_copy(j).start())
    q_fwd(0).start()

    def to_up(b, zb):
        return remote(kv, b, me + 2 * X, up_send.at[zb], kv_recv)

    def to_down(b, zb):
        return remote(kv, b, me - 2 * X, down_send.at[zb], kv_recv)

    def to_x(b, zb, i):
        peer = z * 2 * X + lax.rem(x + i, X) * 2 + c
        return remote(kv, b, peer, x_send.at[zb * X + i], kv_recv)

    def to_sib(b):
        return remote(kv, b, sib, sib_send.at[b // 2], kv_recv)

    def arrived(b):
        remote(kv, b, sib, sib_send.at[0], kv_recv).wait_recv()

    def column(zb):
        return zb * 2 * X + x * 2 + c

    for i in range(1, X):
        to_x(me, z, i).start()

    @pl.when(z + 1 < Z)
    def _():
        to_up(me, z).start()

    @pl.when(z >= 1)
    def _():
        to_down(me, z).start()

    to_sib(me).start()

    def both(*conditions):
        bits = [jnp.where(one, 1, 0) for one in conditions]
        return functools.reduce(lambda p, q: p * q, bits) == 1

    def along_z(h, here):
        below, above = column(z - h), column(z + h)

        @pl.when(both(here, z >= h))
        def _():
            arrived(below)
            for i in range(1, X):
                to_x(below, z - h, i).start()
            to_sib(below).start()

        @pl.when(both(here, z >= h, z + 1 < Z))
        def _():
            to_up(below, z - h).start()

        @pl.when(both(here, z + h < Z))
        def _():
            arrived(above)
            for i in range(1, X):
                to_x(above, z + h, i).start()
            to_sib(above).start()

        @pl.when(both(here, z + h < Z, z >= 1))
        def _():
            to_down(above, z + h).start()

    def pass_on(zb):
        for i in range(1, X):
            b = zb * 2 * X + lax.rem(x + i, X) * 2 + c
            arrived(b)
            to_sib(b).start()

    def across_x(h, here):
        @pl.when(both(here, z >= h))
        def _():
            pass_on(z - h)

        if h > 0:

            @pl.when(both(here, z + h < Z))
            def _():
                pass_on(z + h)

    def q_take(j):
        b = lax.rem(me + 2 * j, n)
        remote(qall, b, sib, q_sib.at[0], q_recv).wait_recv()
        q_fwd(j).start()

    loop(1, half, q_take)

    def q_other(j):
        b = lax.rem(sib + 2 * j, n)
        remote(qall, b, sib, q_sib.at[0], q_recv).wait_recv()

    loop(0, half, q_other)

    lane = lax.broadcasted_iota(jnp.int32, (1, 2 * tok), 1)
    for i in range(half):
        pair = []
        for b in (2 * i, 2 * i + 1):
            coded = qall[b, ROWS:MSG, :].astype(jnp.float32)
            pair.append(coded[0:1] * 128.0 + coded[1:2])
        key_pos[:, i * 2 * tok : (i + 1) * 2 * tok] = jnp.where(lane < tok, pair[0], pair[1])

    for copy in pool_copies:
        copy.wait()

    def attend(q, count, load):
        rows = q.shape[0]

        def chunk(t, carry):
            m, l, acc = carry
            k, v, allowed = load(t)
            s = lax.dot_general(q, k, NT, preferred_element_type=jnp.float32) * SCALE
            s = jnp.where(allowed, s, NEG)
            new = jnp.maximum(m, jnp.max(s, axis=1, keepdims=True))
            w = jnp.exp2(s - new)
            scale = jnp.exp2(m - new)
            l = l * scale + jnp.sum(w, axis=1, keepdims=True)
            acc = acc * scale + jnp.dot(
                w.astype(jnp.bfloat16), v, preferred_element_type=jnp.float32
            )
            return new, l, acc

        carry = (
            jnp.full((rows, 1), NEG, jnp.float32),
            jnp.zeros((rows, 1), jnp.float32),
            jnp.zeros((rows, HD), jnp.float32),
        )
        if count == 1:
            return chunk(0, carry)
        return lax.fori_loop(0, count, chunk, carry)

    chunk_tok = 1024
    drows = SEQ_BLOCK * HEAD_ROWS
    row_seq = lax.broadcasted_iota(jnp.int32, (drows, 1), 0) // HEAD_ROWS
    lane16 = lax.broadcasted_iota(jnp.int32, (HEAD_ROWS, 128), 1)

    def decode_head(h):
        for k in range(1, min(Z, KVH)):
            along_z(k, h == k)
            across_x(k - 1, h == k)

        hrow = pl.multiple_of(h * HEAD_ROWS, HEAD_ROWS)
        hlane = pl.ds(pl.multiple_of(h * HD, HD), HD)

        def seq_block(sb):
            first = sb * SEQ_BLOCK
            q = qall[pl.ds(first, SEQ_BLOCK), pl.ds(hrow, HEAD_ROWS), :].reshape(drows, HD)

            def load(t):
                at = pl.ds(pl.multiple_of(t * chunk_tok, chunk_tok), chunk_tok)
                return pool_k[at, hlane], pool_v[at, hlane], tok_owner[:, at] == row_seq + first

            m, l, acc = attend(q, tokens // chunk_tok, load)
            o = (acc / l).astype(jnp.bfloat16).reshape(SEQ_BLOCK, HEAD_ROWS, HD)
            psend[pl.ds(first, SEQ_BLOCK), pl.ds(hrow, HEAD_ROWS), :] = o
            lse = m + jnp.log2(l)
            seen = stats[pl.ds(hrow, HEAD_ROWS), :]
            for i in range(SEQ_BLOCK):
                seen = jnp.where(
                    lane16 == first + i, lse[i * HEAD_ROWS : (i + 1) * HEAD_ROWS], seen
                )
            stats[pl.ds(hrow, HEAD_ROWS), :] = seen

        loop(0, n // SEQ_BLOCK, seq_block)

    loop(0, KVH, decode_head)

    stats[...] = jnp.transpose(stats[...])
    sub16 = lax.broadcasted_iota(jnp.int32, (16, 128), 0)

    def code(b):
        row = jnp.broadcast_to(stats[pl.ds(b, 1), :], (16, 128))
        hi = row.astype(jnp.bfloat16).astype(jnp.float32)
        mid = (row - hi).astype(jnp.bfloat16).astype(jnp.float32)
        low = row - hi - mid
        coded = jnp.where(sub16 == 0, hi, jnp.where(sub16 == 1, mid, low))
        psend[b, ROWS:MSG, :] = coded.astype(jnp.bfloat16)

    loop(0, n, code)

    def p_copy(j):
        b = lax.rem(me + j, n)
        return pltpu.make_async_remote_copy(
            src_ref=psend.at[b],
            dst_ref=precv.at[me],
            send_sem=p_send.at[j],
            recv_sem=p_recv.at[me],
            device_id={"seq": b},
            device_id_type=MESH,
        )

    loop(1, n, lambda j: p_copy(j).start())
    precv[me] = psend[me]

    for h in range(min(Z, KVH), Z):
        along_z(h, True)
        across_x(h - 1, True)
    across_x(Z - 1, True)

    def kv_other(j):
        arrived(2 * j + 1 - c)

    loop(0, half, kv_other)

    part = 4
    pos_col = jnp.concatenate([row_pos[:, 0:1]] * part, axis=0)
    chunk_keys = 1024
    blocks = chunk_keys // tok

    def prefill(u):
        h = u // (GROUP // part)
        q = jnp.concatenate(
            [
                pq[:, pl.ds(pl.multiple_of((u * part + g) * HD, HD), HD)]
                for g in range(part)
            ],
            axis=0,
        )

        def load(t):
            at = pl.ds(t * blocks, blocks)
            k = kv[at, :, pl.ds(pl.multiple_of(h * HD, HD), HD)].reshape(chunk_keys, HD)
            v = kv[at, :, pl.ds(pl.multiple_of((KVH + h) * HD, HD), HD)].reshape(chunk_keys, HD)
            pos = key_pos[:, pl.ds(pl.multiple_of(t * chunk_keys, chunk_keys), chunk_keys)]
            return k, v, pos <= pos_col

        m, l, acc = attend(q, keys // chunk_keys, load)
        o = (acc / l).astype(jnp.bfloat16)
        for g in range(part):
            out[:, pl.ds(pl.multiple_of((u * part + g) * HD, HD), HD)] = o[g * tok : (g + 1) * tok]

    loop(0, QH // part, prefill)

    def p_take(j):
        b = lax.rem(me + j, n)
        pltpu.make_async_remote_copy(
            src_ref=psend.at[b],
            dst_ref=precv.at[b],
            send_sem=p_send.at[0],
            recv_sem=p_recv.at[b],
            device_id={"seq": b},
            device_id_type=MESH,
        ).wait_recv()

    loop(1, n, p_take)

    def decode_stat(d):
        coded = precv[d, ROWS:MSG, :].astype(jnp.float32)
        stats_in[pl.ds(d, 1), :] = coded[0:1] + coded[1:2] + coded[2:3]

    loop(0, n, decode_stat)
    lse = jnp.transpose(stats_in[...])[0:ROWS]
    q = qmsg[0:ROWS, :].astype(jnp.float32)
    row_id = lax.broadcasted_iota(jnp.int32, (ROWS, 1), 0)
    row_step = (row_id // GROUP) % STEPS
    scores = []
    for j in range(STEPS):
        s = jnp.sum(q * step_k[j], axis=1, keepdims=True) * SCALE
        scores.append(jnp.where(row_step >= j, s, NEG))
    top = jnp.max(lse, axis=1, keepdims=True)
    for s in scores:
        top = jnp.maximum(top, s)
    w = jnp.exp2(lse - top)
    denominator = jnp.sum(w, axis=1, keepdims=True)
    numerator = jnp.zeros((ROWS, HD), jnp.float32)
    for j in range(STEPS):
        e = jnp.exp2(scores[j] - top)
        denominator += e
        numerator += e * step_v[j]
    dev = lax.broadcasted_iota(jnp.int32, (ROWS, 128), 1)

    def add(d, total):
        wd = jnp.sum(jnp.where(dev == d, w, 0.0), axis=1, keepdims=True)
        return total + wd * precv[d, 0:ROWS, :].astype(jnp.float32)

    numerator = lax.fori_loop(0, n, add, numerator, unroll=4)
    dec[...] = (numerator / denominator).astype(jnp.bfloat16)

    loop(1, half, lambda j: q_copy(j).wait_send())
    loop(0, half, lambda j: q_fwd(j).wait_send())
    loop(1, n, lambda j: p_copy(j).wait_send())
    for h in range(Z):

        @pl.when(both(z >= h, z + 1 < Z))
        def _():
            to_up(column(z - h), z - h).wait_send()

        @pl.when(both(z + h < Z, z >= 1))
        def _():
            to_down(column(z + h), z + h).wait_send()

    def left(zb):
        for i in range(1, X):
            to_x(column(zb), zb, i).wait_send()

    loop(0, Z, left)
    loop(0, half, lambda j: to_sib(2 * j + c).wait_send())


def shards(
    prompt_queries,
    prompt_keys,
    prompt_values,
    prompt_positions,
    step_queries,
    step_keys,
    step_values,
    pool_keys,
    pool_values,
    page_owner,
    page_fill,
):
    n = lax.axis_size("seq")
    X = max(1, round((n // 2) ** (1 / 3)))
    Z = n // (2 * X)
    tok = prompt_queries.shape[0]
    pages = pool_keys.shape[0]
    tokens = pages * PAGE
    rows = jnp.transpose(
        step_queries.reshape(STEPS, KVH, GROUP, HD), (1, 0, 2, 3)
    ).reshape(ROWS, HD)
    twice = jnp.concatenate([prompt_positions, prompt_positions])[None]
    coded = jnp.concatenate([twice // 128, twice % 128, jnp.zeros((14, 2 * tok), jnp.int32)])
    qmsg = jnp.concatenate([rows, coded.astype(jnp.bfloat16)])
    row_pos = jnp.broadcast_to(prompt_positions.astype(jnp.float32)[:, None], (tok, 128))
    valid = jnp.arange(PAGE)[None, :] < page_fill[:, None]
    tok_owner = jnp.where(valid, page_owner, -1).reshape(1, tokens)

    def per_row(a):
        a = a.astype(jnp.float32).reshape(STEPS, KVH, 1, HD)
        return jnp.broadcast_to(a, (STEPS, KVH, HEAD_ROWS, HD)).reshape(STEPS, ROWS, HD)

    vmem = pl.BlockSpec(memory_space=pltpu.VMEM)
    hbm = pl.BlockSpec(memory_space=pl.ANY)
    dma = pltpu.SemaphoreType.DMA
    bf16 = jnp.bfloat16
    prefill_out, dec = pl.pallas_call(
        functools.partial(kernel, n, X),
        out_shape=(
            jax.ShapeDtypeStruct((tok, QH * HD), bf16),
            jax.ShapeDtypeStruct((ROWS, HD), bf16),
        ),
        in_specs=[vmem] * 8 + [hbm] * 2,
        out_specs=(vmem, vmem),
        scratch_shapes=[
            pltpu.VMEM((n, MSG, HD), bf16),
            pltpu.VMEM((n, tok, 2 * KVH * HD), bf16),
            pltpu.VMEM((tokens, KVH * HD), bf16),
            pltpu.VMEM((tokens, KVH * HD), bf16),
            pltpu.VMEM((1, n * tok), jnp.float32),
            pltpu.VMEM((n, MSG, HD), bf16),
            pltpu.VMEM((n, MSG, HD), bf16),
            pltpu.VMEM((128, 128), jnp.float32),
            pltpu.VMEM((128, 128), jnp.float32),
            dma((2,)),
            dma((n // 2,)),
            dma((n // 2,)),
            dma((n,)),
            dma((n,)),
            dma((n,)),
            dma((Z,)),
            dma((Z,)),
            dma((Z * X,)),
            dma((n // 2,)),
            dma((n,)),
        ],
        compiler_params=pltpu.CompilerParams(
            collective_id=0, has_side_effects=True, vmem_limit_bytes=56 * 1024 * 1024
        ),
    )(
        qmsg,
        row_pos,
        tok_owner,
        prompt_queries,
        prompt_keys,
        prompt_values,
        per_row(step_keys),
        per_row(step_values),
        pool_keys.reshape(tokens, KVH * HD),
        pool_values.reshape(tokens, KVH * HD),
    )
    decode_out = jnp.transpose(dec.reshape(KVH, STEPS, GROUP, HD), (1, 0, 2, 3))
    return prefill_out, decode_out.reshape(1, STEPS, QH * HD)


def solution(mesh):
    rows = P(("group", "seq"), None)
    flat = P(("group", "seq"))
    cube = P(("group", "seq"), None, None)
    in_specs = (rows, rows, rows, flat, cube, cube, cube, cube, cube, rows, flat)
    return jax.shard_map(
        shards, mesh=mesh, in_specs=in_specs, out_specs=(rows, cube), check_vma=False
    )
```

```python
import functools
import jax
import jax.numpy as jnp
from jax import lax
from jax.experimental import pallas as pl
from jax.experimental.pallas import tpu as pltpu
from jax.sharding import PartitionSpec as P

QH = 32
KVH = 4
HD = 128
GROUP = QH // KVH
PAGE = 128
STEPS = 2
ROWS = STEPS * QH
HEAD_ROWS = STEPS * GROUP
MSG = ROWS + 16
SEQ_BLOCK = 16
NEG = -1e30
LOG2E = 1.4426950408889634
SCALE = HD ** (-0.5) * LOG2E
MESH = pl.DeviceIdType.MESH
NT = (((1,), (1,)), ((), ()))


def kernel(
    n,
    X,
    positions,
    page_owner,
    page_fill,
    step_q,
    pq,
    own_k,
    own_v,
    step_k,
    step_v,
    pool_k_hbm,
    pool_v_hbm,
    out,
    dec,
    qall,
    all_k,
    all_v,
    pool_k,
    pool_v,
    key_pos,
    tok_owner,
    psend,
    precv,
    stats,
    stats_in,
    own_q,
    own_dec,
    run_max,
    run_sum,
    run_out,
    pool_sem,
    q_send,
    q_sib,
    q_recv,
    p_send,
    p_recv,
    up_send,
    down_send,
    x_send,
    sib_send,
    k_recv,
    v_recv,
):
    Z = n // (2 * X)
    half = n // 2
    me = lax.axis_index("seq")
    c = lax.rem(me, 2)
    x = lax.rem(me // 2, X)
    z = me // (2 * X)
    sib = me + 1 - 2 * c
    tok = own_k.shape[0]
    keys = n * tok
    tokens = pool_k.shape[0]

    pool_copies = [
        pltpu.make_async_copy(pool_k_hbm, pool_k, pool_sem.at[0]),
        pltpu.make_async_copy(pool_v_hbm, pool_v, pool_sem.at[1]),
    ]
    barrier = pltpu.get_barrier_semaphore()

    def greet(i, carry):
        pl.semaphore_signal(
            barrier, inc=1, device_id={"seq": lax.rem(me + i, n)}, device_id_type=MESH
        )
        return carry

    lax.fori_loop(1, n, greet, 0)
    for copy in pool_copies:
        copy.start()
    all_k[me] = own_k[...]
    all_v[me] = own_v[...]
    wide_q = step_q[0].astype(jnp.float32)
    for j in range(QH):
        for i in range(STEPS):
            r = (j // GROUP) * HEAD_ROWS + i * GROUP + j % GROUP
            own_q[r : r + 1, :] = wide_q[i : i + 1, j * HD : (j + 1) * HD]
    qall[me, 0:ROWS, :] = own_q[...].astype(jnp.bfloat16)

    def row_position(i):
        return jnp.where(i < tok // 2, positions[0] + i, positions[tok // 2] + i - tok // 2)

    sub16 = lax.broadcasted_iota(jnp.int32, (16, 128), 0)
    lane_pos = row_position(lax.broadcasted_iota(jnp.int32, (16, 128), 1) % tok)
    coded = jnp.where(sub16 == 0, lane_pos // 128, lane_pos % 128)
    qall[me, ROWS:MSG, :] = coded.astype(jnp.float32).astype(jnp.bfloat16)
    stats[...] = jnp.full_like(stats, NEG)
    stats_in[...] = jnp.full_like(stats_in, NEG)
    pl.semaphore_wait(barrier, n - 1)

    def remote(buf, b, peer, ss, rs):
        return pltpu.make_async_remote_copy(
            src_ref=buf.at[b],
            dst_ref=buf.at[b],
            send_sem=ss,
            recv_sem=rs.at[b],
            device_id={"seq": peer},
            device_id_type=MESH,
        )

    def q_copy(j):
        return remote(qall, me, lax.rem(me + 2 * j, n), q_send.at[j], q_recv)

    def q_fwd(j):
        b = lax.rem(me + 2 * j, n)
        return remote(qall, b, sib, q_sib.at[j], q_recv)

    def loop(lo, hi, body):
        def step(i, carry):
            body(i)
            return carry

        lax.fori_loop(lo, hi, step, 0)

    loop(1, half, lambda j: q_copy(j).start())
    q_fwd(0).start()

    parts = ((0, all_k, k_recv), (1, all_v, v_recv))

    def to_up(b, zb, part):
        i, buf, rs = part
        return remote(buf, b, me + 2 * X, up_send.at[2 * zb + i], rs)

    def to_down(b, zb, part):
        i, buf, rs = part
        return remote(buf, b, me - 2 * X, down_send.at[2 * zb + i], rs)

    def to_x(b, zb, j, part):
        i, buf, rs = part
        peer = z * 2 * X + lax.rem(x + j, X) * 2 + c
        return remote(buf, b, peer, x_send.at[(zb * X + j) * 2 + i], rs)

    def to_sib(b, part):
        i, buf, rs = part
        return remote(buf, b, sib, sib_send.at[b // 2 * 2 + i], rs)

    def arrived(b, part):
        i, buf, rs = part
        remote(buf, b, sib, sib_send.at[i], rs).wait_recv()

    def column(zb):
        return zb * 2 * X + x * 2 + c

    def both(*conditions):
        bits = [jnp.where(one, 1, 0) for one in conditions]
        return functools.reduce(lambda p, q: p * q, bits) == 1

    for part in parts:

        @pl.when(z + 1 < Z)
        def _():
            to_up(me, z, part).start()

        @pl.when(z >= 1)
        def _():
            to_down(me, z, part).start()

        for j in range(1, X):
            to_x(me, z, j, part).start()
        to_sib(me, part).start()

    def along_z(h, here):
        below, above = column(z - h), column(z + h)
        for part in parts:

            @pl.when(both(here, z >= h))
            def _():
                arrived(below, part)

            @pl.when(both(here, z >= h, z + 1 < Z))
            def _():
                to_up(below, z - h, part).start()

            @pl.when(both(here, z >= h))
            def _():
                for j in range(1, X):
                    to_x(below, z - h, j, part).start()
                to_sib(below, part).start()

            @pl.when(both(here, z + h < Z))
            def _():
                arrived(above, part)

            @pl.when(both(here, z + h < Z, z >= 1))
            def _():
                to_down(above, z + h, part).start()

            @pl.when(both(here, z + h < Z))
            def _():
                for j in range(1, X):
                    to_x(above, z + h, j, part).start()
                to_sib(above, part).start()

    def pass_on(zb, part):
        for j in range(1, X):
            b = zb * 2 * X + lax.rem(x + j, X) * 2 + c
            arrived(b, part)
            to_sib(b, part).start()

    def across_x(h, here):
        for part in parts:

            @pl.when(both(here, z >= h))
            def _():
                pass_on(z - h, part)

            if h > 0:

                @pl.when(both(here, z + h < Z))
                def _():
                    pass_on(z + h, part)

    def q_take(j):
        b = lax.rem(me + 2 * j, n)
        remote(qall, b, sib, q_sib.at[0], q_recv).wait_recv()
        q_fwd(j).start()

    loop(1, half, q_take)

    def q_other(j):
        b = lax.rem(sib + 2 * j, n)
        remote(qall, b, sib, q_sib.at[0], q_recv).wait_recv()

    loop(0, half, q_other)

    lane = lax.broadcasted_iota(jnp.int32, (1, 2 * tok), 1)
    for i in range(half):
        pair = []
        for b in (2 * i, 2 * i + 1):
            coded = qall[b, ROWS:MSG, :].astype(jnp.float32)
            pair.append(coded[0:1] * 128.0 + coded[1:2])
        key_pos[:, i * 2 * tok : (i + 1) * 2 * tok] = jnp.where(lane < tok, pair[0], pair[1])

    page_lane = lax.broadcasted_iota(jnp.int32, (1, PAGE), 1)
    for p in range(tokens // PAGE):
        tok_owner[:, p * PAGE : (p + 1) * PAGE] = jnp.where(
            page_lane < page_fill[p], page_owner[p], -1
        )

    for copy in pool_copies:
        copy.wait()

    def fold(q, k, v, allowed, m, l, acc):
        s = lax.dot_general(q, k, NT, preferred_element_type=jnp.float32) * SCALE
        s = jnp.where(allowed, s, NEG)
        new = jnp.maximum(m, jnp.max(s, axis=1, keepdims=True))
        w = jnp.exp2(s - new)
        scale = jnp.exp2(m - new)
        l = l * scale + jnp.sum(w, axis=1, keepdims=True)
        acc = acc * scale + jnp.dot(
            w.astype(jnp.bfloat16), v, preferred_element_type=jnp.float32
        )
        return new, l, acc

    def empty(rows):
        return (
            jnp.full((rows, 1), NEG, jnp.float32),
            jnp.zeros((rows, 1), jnp.float32),
            jnp.zeros((rows, HD), jnp.float32),
        )

    chunk_tok = 1024
    drows = SEQ_BLOCK * HEAD_ROWS
    row_seq = lax.broadcasted_iota(jnp.int32, (drows, 1), 0) // HEAD_ROWS
    lane16 = lax.broadcasted_iota(jnp.int32, (HEAD_ROWS, 128), 1)

    def decode_head(h):
        for k in range(1, min(Z, KVH - 1)):
            along_z(k, h == k)
            across_x(k - 1, h == k)

        hrow = pl.multiple_of(h * HEAD_ROWS, HEAD_ROWS)
        hlane = pl.ds(pl.multiple_of(h * HD, HD), HD)

        def seq_block(sb):
            first = sb * SEQ_BLOCK
            q = qall[pl.ds(first, SEQ_BLOCK), pl.ds(hrow, HEAD_ROWS), :].reshape(drows, HD)

            def chunk(t, carry):
                at = pl.ds(pl.multiple_of(t * chunk_tok, chunk_tok), chunk_tok)
                allowed = tok_owner[:, at] == row_seq + first
                return fold(q, pool_k[at, hlane], pool_v[at, hlane], allowed, *carry)

            m, l, acc = lax.fori_loop(0, tokens // chunk_tok, chunk, empty(drows))
            o = (acc / l).astype(jnp.bfloat16).reshape(SEQ_BLOCK, HEAD_ROWS, HD)
            psend[pl.ds(first, SEQ_BLOCK), pl.ds(hrow, HEAD_ROWS), :] = o
            lse = m + jnp.log2(l)
            seen = stats[pl.ds(hrow, HEAD_ROWS), :]
            for i in range(SEQ_BLOCK):
                seen = jnp.where(
                    lane16 == first + i, lse[i * HEAD_ROWS : (i + 1) * HEAD_ROWS], seen
                )
            stats[pl.ds(hrow, HEAD_ROWS), :] = seen

        loop(0, n // SEQ_BLOCK, seq_block)

    loop(0, KVH, decode_head)

    stats[...] = jnp.transpose(stats[...])
    def code(b):
        row = jnp.broadcast_to(stats[pl.ds(b, 1), :], (16, 128))
        hi = row.astype(jnp.bfloat16).astype(jnp.float32)
        mid = (row - hi).astype(jnp.bfloat16).astype(jnp.float32)
        low = row - hi - mid
        coded = jnp.where(sub16 == 0, hi, jnp.where(sub16 == 1, mid, low))
        psend[b, ROWS:MSG, :] = coded.astype(jnp.bfloat16)

    loop(0, n, code)

    def p_copy(j):
        b = lax.rem(me + j, n)
        return pltpu.make_async_remote_copy(
            src_ref=psend.at[b],
            dst_ref=precv.at[me],
            send_sem=p_send.at[j],
            recv_sem=p_recv.at[me],
            device_id={"seq": b},
            device_id_type=MESH,
        )

    loop(1, n, lambda j: p_copy(j).start())
    precv[me] = psend[me]

    prows = GROUP * tok
    pos_col = jnp.concatenate(
        [row_position(lax.broadcasted_iota(jnp.int32, (tok, 1), 0)).astype(jnp.float32)] * GROUP,
        axis=0,
    )
    blocks = 2 * X
    chunk_keys = blocks * tok
    nearest = [sorted(range(Z), key=lambda w: (abs(w - zz), w)) for zz in range(Z)]

    def prefill(k):
        zk = sum(jnp.where(z == zz, nearest[zz][k], 0) for zz in range(Z))
        for part in parts:
            for j in range(X):
                arrived(zk * blocks + 2 * j + 1 - c, part)
        at = pl.ds(zk * blocks, blocks)
        pos = key_pos[:, pl.ds(pl.multiple_of(zk * chunk_keys, chunk_keys), chunk_keys)]

        def head(h):
            lanes = pl.ds(pl.multiple_of(h * HD, HD), HD)
            q = jnp.concatenate(
                [
                    pq[:, pl.ds(pl.multiple_of((h * GROUP + g) * HD, HD), HD)]
                    for g in range(GROUP)
                ],
                axis=0,
            )
            key = all_k[at, :, lanes].reshape(chunk_keys, HD)
            value = all_v[at, :, lanes].reshape(chunk_keys, HD)
            rows = pl.ds(pl.multiple_of(h * prows, prows), prows)
            carry = empty(prows) if k == 0 else (run_max[rows], run_sum[rows], run_out[rows])
            m, l, acc = fold(q, key, value, pos <= pos_col, *carry)
            if k < Z - 1:
                run_max[rows], run_sum[rows], run_out[rows] = m, l, acc
                return
            o = (acc / l).astype(jnp.bfloat16)
            for g in range(GROUP):
                out[:, pl.ds(pl.multiple_of((h * GROUP + g) * HD, HD), HD)] = o[
                    g * tok : (g + 1) * tok
                ]

        loop(0, KVH, head)

    done = min(Z, KVH - 1) - 1
    for k in range(Z):
        if k > done:
            along_z(k, True)
            across_x(k - 1, True)
        if k == Z - 1:
            across_x(k, True)
        prefill(k)
        if k == 0 and done + 1 < Z:
            done += 1
            along_z(done, True)
            across_x(done - 1, True)

    def p_take(j):
        b = lax.rem(me + j, n)
        pltpu.make_async_remote_copy(
            src_ref=psend.at[b],
            dst_ref=precv.at[b],
            send_sem=p_send.at[0],
            recv_sem=p_recv.at[b],
            device_id={"seq": b},
            device_id_type=MESH,
        ).wait_recv()

    loop(1, n, p_take)

    def decode_stat(d):
        coded = precv[d, ROWS:MSG, :].astype(jnp.float32)
        stats_in[pl.ds(d, 1), :] = coded[0:1] + coded[1:2] + coded[2:3]

    loop(0, n, decode_stat)
    lse = jnp.transpose(stats_in[...])[0:ROWS]
    q = own_q[...]
    row_id = lax.broadcasted_iota(jnp.int32, (ROWS, 1), 0)
    row_step = (row_id // GROUP) % STEPS

    def per_row(wide, j):
        return jnp.concatenate(
            [
                jnp.broadcast_to(wide[j : j + 1, h * HD : (h + 1) * HD], (HEAD_ROWS, HD))
                for h in range(KVH)
            ],
            axis=0,
        )

    wide_k = step_k[0].astype(jnp.float32)
    wide_v = step_v[0].astype(jnp.float32)
    scores = []
    for j in range(STEPS):
        s = jnp.sum(q * per_row(wide_k, j), axis=1, keepdims=True) * SCALE
        scores.append(jnp.where(row_step >= j, s, NEG))
    top = jnp.max(lse, axis=1, keepdims=True)
    for s in scores:
        top = jnp.maximum(top, s)
    w = jnp.exp2(lse - top)
    denominator = jnp.sum(w, axis=1, keepdims=True)
    numerator = jnp.zeros((ROWS, HD), jnp.float32)
    for j in range(STEPS):
        e = jnp.exp2(scores[j] - top)
        denominator += e
        numerator += e * per_row(wide_v, j)
    dev = lax.broadcasted_iota(jnp.int32, (ROWS, 128), 1)

    def add(d, total):
        wd = jnp.sum(jnp.where(dev == d, w, 0.0), axis=1, keepdims=True)
        return total + wd * precv[d, 0:ROWS, :].astype(jnp.float32)

    numerator = lax.fori_loop(0, n, add, numerator, unroll=4)
    result = numerator / denominator
    for j in range(QH):
        for i in range(STEPS):
            r = (j // GROUP) * HEAD_ROWS + i * GROUP + j % GROUP
            own_dec[i : i + 1, j * HD : (j + 1) * HD] = result[r : r + 1]
    dec[0] = own_dec[...].astype(jnp.bfloat16)

    loop(1, half, lambda j: q_copy(j).wait_send())
    loop(0, half, lambda j: q_fwd(j).wait_send())
    loop(1, n, lambda j: p_copy(j).wait_send())
    for part in parts:
        for h in range(Z):

            @pl.when(both(z >= h, z + 1 < Z))
            def _():
                to_up(column(z - h), z - h, part).wait_send()

            @pl.when(both(z + h < Z, z >= 1))
            def _():
                to_down(column(z + h), z + h, part).wait_send()

        def left(zb):
            for j in range(1, X):
                to_x(column(zb), zb, j, part).wait_send()

        loop(0, Z, left)
        loop(0, half, lambda j: to_sib(2 * j + c, part).wait_send())


def shards(
    prompt_queries,
    prompt_keys,
    prompt_values,
    prompt_positions,
    step_queries,
    step_keys,
    step_values,
    pool_keys,
    pool_values,
    page_owner,
    page_fill,
):
    n = lax.axis_size("seq")
    X = max(1, round((n // 2) ** (1 / 3)))
    Z = n // (2 * X)
    tok = prompt_queries.shape[0]
    pages = pool_keys.shape[0]
    tokens = pages * PAGE
    vmem = pl.BlockSpec(memory_space=pltpu.VMEM)
    smem = pl.BlockSpec(memory_space=pltpu.SMEM)
    hbm = pl.BlockSpec(memory_space=pl.ANY)
    dma = pltpu.SemaphoreType.DMA
    bf16 = jnp.bfloat16
    return pl.pallas_call(
        functools.partial(kernel, n, X),
        out_shape=(
            jax.ShapeDtypeStruct((tok, QH * HD), bf16),
            jax.ShapeDtypeStruct((1, STEPS, QH * HD), bf16),
        ),
        in_specs=[smem] * 3 + [vmem] * 6 + [hbm] * 2,
        out_specs=(vmem, vmem),
        scratch_shapes=[
            pltpu.VMEM((n, MSG, HD), bf16),
            pltpu.VMEM((n, tok, KVH * HD), bf16),
            pltpu.VMEM((n, tok, KVH * HD), bf16),
            pltpu.VMEM((tokens, KVH * HD), bf16),
            pltpu.VMEM((tokens, KVH * HD), bf16),
            pltpu.VMEM((1, n * tok), jnp.float32),
            pltpu.VMEM((1, tokens), jnp.int32),
            pltpu.VMEM((n, MSG, HD), bf16),
            pltpu.VMEM((n, MSG, HD), bf16),
            pltpu.VMEM((128, 128), jnp.float32),
            pltpu.VMEM((128, 128), jnp.float32),
            pltpu.VMEM((ROWS, HD), jnp.float32),
            pltpu.VMEM((STEPS, QH * HD), jnp.float32),
            pltpu.VMEM((QH * tok, 1), jnp.float32),
            pltpu.VMEM((QH * tok, 1), jnp.float32),
            pltpu.VMEM((QH * tok, HD), jnp.float32),
            dma((2,)),
            dma((n // 2,)),
            dma((n // 2,)),
            dma((n,)),
            dma((n,)),
            dma((n,)),
            dma((2 * Z,)),
            dma((2 * Z,)),
            dma((2 * Z * X,)),
            dma((n,)),
            dma((n,)),
            dma((n,)),
        ],
        compiler_params=pltpu.CompilerParams(
            collective_id=0, has_side_effects=True, vmem_limit_bytes=56 * 1024 * 1024
        ),
    )(
        prompt_positions,
        page_owner.reshape(pages),
        page_fill,
        step_queries,
        prompt_queries,
        prompt_keys,
        prompt_values,
        step_keys,
        step_values,
        pool_keys.reshape(tokens, KVH * HD),
        pool_values.reshape(tokens, KVH * HD),
    )


def solution(mesh):
    rows = P(("group", "seq"), None)
    flat = P(("group", "seq"))
    cube = P(("group", "seq"), None, None)
    in_specs = (rows, rows, rows, flat, cube, cube, cube, cube, cube, rows, flat)
    return jax.shard_map(
        shards, mesh=mesh, in_specs=in_specs, out_specs=(rows, cube), check_vma=False
    )
```

```python
import functools
import jax
import jax.numpy as jnp
from jax import lax
from jax.experimental import pallas as pl
from jax.experimental.pallas import tpu as pltpu
from jax.sharding import PartitionSpec as P

QH = 32
KVH = 4
HD = 128
GROUP = QH // KVH
PAGE = 128
STEPS = 2
ROWS = STEPS * QH
HEAD_ROWS = STEPS * GROUP
MSG = ROWS + 16
SEQ_BLOCK = 16
NEG = -1e30
LOG2E = 1.4426950408889634
SCALE = HD ** (-0.5) * LOG2E
MESH = pl.DeviceIdType.MESH
NT = (((1,), (1,)), ((), ()))


def kernel(
    n,
    X,
    positions,
    page_owner,
    page_fill,
    step_q,
    pq,
    own_k,
    own_v,
    step_k,
    step_v,
    pool_k_hbm,
    pool_v_hbm,
    out,
    dec,
    qall,
    all_k,
    all_v,
    pool_k,
    pool_v,
    key_pos,
    tok_owner,
    psend,
    precv,
    stats,
    stats_in,
    own_q,
    own_dec,
    pool_sem,
    q_send,
    q_sib,
    q_recv,
    p_send,
    p_recv,
    up_send,
    down_send,
    x_send,
    sib_send,
    k_recv,
    v_recv,
):
    Z = n // (2 * X)
    half = n // 2
    me = lax.axis_index("seq")
    c = lax.rem(me, 2)
    x = lax.rem(me // 2, X)
    z = me // (2 * X)
    sib = me + 1 - 2 * c
    tok = own_k.shape[0]
    tokens = pool_k.shape[0]

    pool_copies = [
        pltpu.make_async_copy(pool_k_hbm, pool_k, pool_sem.at[0]),
        pltpu.make_async_copy(pool_v_hbm, pool_v, pool_sem.at[1]),
    ]
    barrier = pltpu.get_barrier_semaphore()

    def greet(i, carry):
        pl.semaphore_signal(
            barrier, inc=1, device_id={"seq": lax.rem(me + i, n)}, device_id_type=MESH
        )
        return carry

    lax.fori_loop(1, n, greet, 0)
    for copy in pool_copies:
        copy.start()
    all_k[me] = own_k[...]
    all_v[me] = own_v[...]
    wide_q = step_q[0].astype(jnp.float32)
    for j in range(QH):
        for i in range(STEPS):
            r = (j // GROUP) * HEAD_ROWS + i * GROUP + j % GROUP
            own_q[r : r + 1, :] = wide_q[i : i + 1, j * HD : (j + 1) * HD]
    qall[me, 0:ROWS, :] = own_q[...].astype(jnp.bfloat16)

    def row_position(i):
        return jnp.where(i < tok // 2, positions[0] + i, positions[tok // 2] + i - tok // 2)

    sub16 = lax.broadcasted_iota(jnp.int32, (16, 128), 0)
    lane_pos = row_position(lax.broadcasted_iota(jnp.int32, (16, 128), 1) % tok)
    coded = jnp.where(sub16 == 0, lane_pos // 128, lane_pos % 128)
    qall[me, ROWS:MSG, :] = coded.astype(jnp.float32).astype(jnp.bfloat16)
    stats[...] = jnp.full_like(stats, NEG)
    stats_in[...] = jnp.full_like(stats_in, NEG)
    pl.semaphore_wait(barrier, n - 1)

    def remote(buf, b, peer, ss, rs):
        return pltpu.make_async_remote_copy(
            src_ref=buf.at[b],
            dst_ref=buf.at[b],
            send_sem=ss,
            recv_sem=rs.at[b],
            device_id={"seq": peer},
            device_id_type=MESH,
        )

    def q_copy(j):
        return remote(qall, me, lax.rem(me + 2 * j, n), q_send.at[j], q_recv)

    def q_fwd(j):
        b = lax.rem(me + 2 * j, n)
        return remote(qall, b, sib, q_sib.at[j], q_recv)

    def loop(lo, hi, body):
        def step(i, carry):
            body(i)
            return carry

        lax.fori_loop(lo, hi, step, 0)

    loop(1, half, lambda j: q_copy(j).start())
    q_fwd(0).start()

    parts = ((0, all_k, k_recv), (1, all_v, v_recv))

    def to_up(b, zb, part):
        i, buf, rs = part
        return remote(buf, b, me + 2 * X, up_send.at[2 * zb + i], rs)

    def to_down(b, zb, part):
        i, buf, rs = part
        return remote(buf, b, me - 2 * X, down_send.at[2 * zb + i], rs)

    def to_x(b, zb, j, part):
        i, buf, rs = part
        peer = z * 2 * X + lax.rem(x + j, X) * 2 + c
        return remote(buf, b, peer, x_send.at[(zb * X + j) * 2 + i], rs)

    def to_sib(b, part):
        i, buf, rs = part
        return remote(buf, b, sib, sib_send.at[b // 2 * 2 + i], rs)

    def arrived(b, part):
        i, buf, rs = part
        remote(buf, b, sib, sib_send.at[i], rs).wait_recv()

    def column(zb):
        return zb * 2 * X + x * 2 + c

    def both(*conditions):
        bits = [jnp.where(one, 1, 0) for one in conditions]
        return functools.reduce(lambda p, q: p * q, bits) == 1

    def along_z(h, here):
        below, above = column(z - h), column(z + h)
        for part in parts:

            @pl.when(both(here, z >= h))
            def _():
                arrived(below, part)

            @pl.when(both(here, z >= h, z + 1 < Z))
            def _():
                to_up(below, z - h, part).start()

            @pl.when(both(here, z >= h))
            def _():
                for j in range(1, X):
                    to_x(below, z - h, j, part).start()
                to_sib(below, part).start()

            @pl.when(both(here, z + h < Z))
            def _():
                arrived(above, part)

            @pl.when(both(here, z + h < Z, z >= 1))
            def _():
                to_down(above, z + h, part).start()

            @pl.when(both(here, z + h < Z))
            def _():
                for j in range(1, X):
                    to_x(above, z + h, j, part).start()
                to_sib(above, part).start()

    def pass_on(zb, part):
        for j in range(1, X):
            b = zb * 2 * X + lax.rem(x + j, X) * 2 + c
            arrived(b, part)
            to_sib(b, part).start()

    def across_x(h, here):
        for part in parts:

            @pl.when(both(here, z >= h))
            def _():
                pass_on(z - h, part)

            if h > 0:

                @pl.when(both(here, z + h < Z))
                def _():
                    pass_on(z + h, part)

    def q_take(j):
        b = lax.rem(me + 2 * j, n)
        remote(qall, b, sib, q_sib.at[0], q_recv).wait_recv()
        q_fwd(j).start()

    loop(1, half, q_take)

    for part in parts:

        @pl.when(z + 1 < Z)
        def _():
            to_up(me, z, part).start()

        @pl.when(z >= 1)
        def _():
            to_down(me, z, part).start()

        for j in range(1, X):
            to_x(me, z, j, part).start()
        to_sib(me, part).start()

    def q_other(j):
        b = lax.rem(sib + 2 * j, n)
        remote(qall, b, sib, q_sib.at[0], q_recv).wait_recv()

    loop(0, half, q_other)

    lane = lax.broadcasted_iota(jnp.int32, (1, 2 * tok), 1)
    for i in range(half):
        pair = []
        for b in (2 * i, 2 * i + 1):
            coded = qall[b, ROWS:MSG, :].astype(jnp.float32)
            pair.append(coded[0:1] * 128.0 + coded[1:2])
        key_pos[:, i * 2 * tok : (i + 1) * 2 * tok] = jnp.where(lane < tok, pair[0], pair[1])

    page_lane = lax.broadcasted_iota(jnp.int32, (1, PAGE), 1)
    for p in range(tokens // PAGE):
        tok_owner[:, p * PAGE : (p + 1) * PAGE] = jnp.where(
            page_lane < page_fill[p], page_owner[p], -1
        )

    for copy in pool_copies:
        copy.wait()

    def fold(q, k, v, allowed, m, acc):
        s = lax.dot_general(q, k, NT, preferred_element_type=jnp.float32) * SCALE
        s = jnp.where(allowed, s, NEG)
        new = jnp.max(s, axis=1, keepdims=True)
        if m is not None:
            new = jnp.maximum(m, new)
        w = jnp.exp2(s - new).astype(jnp.bfloat16)
        wide = jnp.concatenate([v, jnp.ones_like(v)], axis=1)
        more = jnp.dot(w, wide, preferred_element_type=jnp.float32)
        return new, more if m is None else acc * jnp.exp2(m - new) + more

    chunk_tok = 512
    drows = SEQ_BLOCK * HEAD_ROWS
    row_seq = lax.broadcasted_iota(jnp.int32, (drows, 1), 0) // HEAD_ROWS
    lane16 = lax.broadcasted_iota(jnp.int32, (HEAD_ROWS, 128), 1)

    def decode_head(h):
        for k in range(1, min(Z, KVH)):
            along_z(k, h == k)
            across_x(k - 1, h == k)

        hrow = pl.multiple_of(h * HEAD_ROWS, HEAD_ROWS)
        hlane = pl.ds(pl.multiple_of(h * HD, HD), HD)

        def seq_block(sb):
            first = sb * SEQ_BLOCK
            q = qall[pl.ds(first, SEQ_BLOCK), pl.ds(hrow, HEAD_ROWS), :].reshape(drows, HD)

            def chunk(t, carry):
                at = pl.ds(t * chunk_tok, chunk_tok)
                allowed = tok_owner[:, at] == row_seq + first
                return fold(q, pool_k[at, hlane], pool_v[at, hlane], allowed, *carry)

            carry = (None, None)
            for t in range(tokens // chunk_tok):
                carry = chunk(t, carry)
            m, acc = carry
            l = acc[:, HD : HD + 1]
            o = (acc[:, :HD] / acc[:, HD:]).astype(jnp.bfloat16).reshape(SEQ_BLOCK, HEAD_ROWS, HD)
            psend[pl.ds(first, SEQ_BLOCK), pl.ds(hrow, HEAD_ROWS), :] = o
            lse = m + jnp.log2(l)
            seen = stats[pl.ds(hrow, HEAD_ROWS), :]
            for i in range(SEQ_BLOCK):
                seen = jnp.where(
                    lane16 == first + i, lse[i * HEAD_ROWS : (i + 1) * HEAD_ROWS], seen
                )
            stats[pl.ds(hrow, HEAD_ROWS), :] = seen

        loop(0, n // SEQ_BLOCK, seq_block)

    loop(0, KVH, decode_head)

    stats[...] = jnp.transpose(stats[...])
    def code(b):
        row = jnp.broadcast_to(stats[pl.ds(b, 1), :], (16, 128))
        hi = row.astype(jnp.bfloat16).astype(jnp.float32)
        mid = (row - hi).astype(jnp.bfloat16).astype(jnp.float32)
        low = row - hi - mid
        coded = jnp.where(sub16 == 0, hi, jnp.where(sub16 == 1, mid, low))
        psend[b, ROWS:MSG, :] = coded.astype(jnp.bfloat16)

    loop(0, n, code)

    def p_copy(j):
        b = lax.rem(me + j, n)
        return pltpu.make_async_remote_copy(
            src_ref=psend.at[b],
            dst_ref=precv.at[me],
            send_sem=p_send.at[j],
            recv_sem=p_recv.at[me],
            device_id={"seq": b},
            device_id_type=MESH,
        )

    loop(1, n, lambda j: p_copy(j).start())
    precv[me] = psend[me]

    for h in range(min(Z, KVH), Z):
        along_z(h, True)
        across_x(h - 1, True)
    across_x(Z - 1, True)

    def kv_other(j):
        for part in parts:
            arrived(2 * j + 1 - c, part)

    loop(0, half, kv_other)

    fan = 8
    pos_col = jnp.concatenate(
        [row_position(lax.broadcasted_iota(jnp.int32, (tok, 1), 0)).astype(jnp.float32)] * fan,
        axis=0,
    )
    chunk_keys = 1024
    blocks = chunk_keys // tok

    def prefill(u):
        h = u // (GROUP // fan)
        lanes = pl.ds(pl.multiple_of(h * HD, HD), HD)
        q = jnp.concatenate(
            [pq[:, pl.ds(pl.multiple_of((u * fan + g) * HD, HD), HD)] for g in range(fan)],
            axis=0,
        )
        carry = (None, None)
        for t in range(n * tok // chunk_keys):
            at = pl.ds(t * blocks, blocks)
            key = all_k[at, :, lanes].reshape(chunk_keys, HD)
            value = all_v[at, :, lanes].reshape(chunk_keys, HD)
            pos = key_pos[:, pl.ds(t * chunk_keys, chunk_keys)]
            carry = fold(q, key, value, pos <= pos_col, *carry)
        acc = carry[1]
        o = (acc[:, :HD] / acc[:, HD:]).astype(jnp.bfloat16)
        for g in range(fan):
            out[:, pl.ds(pl.multiple_of((u * fan + g) * HD, HD), HD)] = o[g * tok : (g + 1) * tok]

    loop(0, QH // fan, prefill)

    def p_take(j):
        b = lax.rem(me + j, n)
        pltpu.make_async_remote_copy(
            src_ref=psend.at[b],
            dst_ref=precv.at[b],
            send_sem=p_send.at[0],
            recv_sem=p_recv.at[b],
            device_id={"seq": b},
            device_id_type=MESH,
        ).wait_recv()

    loop(1, n, p_take)

    def decode_stat(d):
        coded = precv[d, ROWS:MSG, :].astype(jnp.float32)
        stats_in[pl.ds(d, 1), :] = coded[0:1] + coded[1:2] + coded[2:3]

    loop(0, n, decode_stat)
    lse = jnp.transpose(stats_in[...])[0:ROWS]
    q = own_q[...]
    row_id = lax.broadcasted_iota(jnp.int32, (ROWS, 1), 0)
    row_step = (row_id // GROUP) % STEPS

    def per_row(wide, j):
        return jnp.concatenate(
            [
                jnp.broadcast_to(wide[j : j + 1, h * HD : (h + 1) * HD], (HEAD_ROWS, HD))
                for h in range(KVH)
            ],
            axis=0,
        )

    wide_k = step_k[0].astype(jnp.float32)
    wide_v = step_v[0].astype(jnp.float32)
    scores = []
    for j in range(STEPS):
        s = jnp.sum(q * per_row(wide_k, j), axis=1, keepdims=True) * SCALE
        scores.append(jnp.where(row_step >= j, s, NEG))
    top = jnp.max(lse, axis=1, keepdims=True)
    for s in scores:
        top = jnp.maximum(top, s)
    w = jnp.exp2(lse - top)
    denominator = jnp.sum(w, axis=1, keepdims=True)
    numerator = jnp.zeros((ROWS, HD), jnp.float32)
    for j in range(STEPS):
        e = jnp.exp2(scores[j] - top)
        denominator += e
        numerator += e * per_row(wide_v, j)
    dev = lax.broadcasted_iota(jnp.int32, (ROWS, 128), 1)

    def add(d, total):
        wd = jnp.sum(jnp.where(dev == d, w, 0.0), axis=1, keepdims=True)
        return total + wd * precv[d, 0:ROWS, :].astype(jnp.float32)

    numerator = lax.fori_loop(0, n, add, numerator, unroll=4)
    result = numerator / denominator
    for j in range(QH):
        for i in range(STEPS):
            r = (j // GROUP) * HEAD_ROWS + i * GROUP + j % GROUP
            own_dec[i : i + 1, j * HD : (j + 1) * HD] = result[r : r + 1]
    dec[0] = own_dec[...].astype(jnp.bfloat16)

    loop(1, half, lambda j: q_copy(j).wait_send())
    loop(0, half, lambda j: q_fwd(j).wait_send())
    loop(1, n, lambda j: p_copy(j).wait_send())
    for part in parts:
        for h in range(Z):

            @pl.when(both(z >= h, z + 1 < Z))
            def _():
                to_up(column(z - h), z - h, part).wait_send()

            @pl.when(both(z + h < Z, z >= 1))
            def _():
                to_down(column(z + h), z + h, part).wait_send()

        def left(zb):
            for j in range(1, X):
                to_x(column(zb), zb, j, part).wait_send()

        loop(0, Z, left)
        loop(0, half, lambda j: to_sib(2 * j + c, part).wait_send())


def shards(
    prompt_queries,
    prompt_keys,
    prompt_values,
    prompt_positions,
    step_queries,
    step_keys,
    step_values,
    pool_keys,
    pool_values,
    page_owner,
    page_fill,
):
    n = lax.axis_size("seq")
    X = max(1, round((n // 2) ** (1 / 3)))
    Z = n // (2 * X)
    tok = prompt_queries.shape[0]
    pages = pool_keys.shape[0]
    tokens = pages * PAGE
    vmem = pl.BlockSpec(memory_space=pltpu.VMEM)
    smem = pl.BlockSpec(memory_space=pltpu.SMEM)
    hbm = pl.BlockSpec(memory_space=pl.ANY)
    dma = pltpu.SemaphoreType.DMA
    bf16 = jnp.bfloat16
    return pl.pallas_call(
        functools.partial(kernel, n, X),
        out_shape=(
            jax.ShapeDtypeStruct((tok, QH * HD), bf16),
            jax.ShapeDtypeStruct((1, STEPS, QH * HD), bf16),
        ),
        in_specs=[smem] * 3 + [vmem] * 6 + [hbm] * 2,
        out_specs=(vmem, vmem),
        scratch_shapes=[
            pltpu.VMEM((n, MSG, HD), bf16),
            pltpu.VMEM((n, tok, KVH * HD), bf16),
            pltpu.VMEM((n, tok, KVH * HD), bf16),
            pltpu.VMEM((tokens, KVH * HD), bf16),
            pltpu.VMEM((tokens, KVH * HD), bf16),
            pltpu.VMEM((1, n * tok), jnp.float32),
            pltpu.VMEM((1, tokens), jnp.int32),
            pltpu.VMEM((n, MSG, HD), bf16),
            pltpu.VMEM((n, MSG, HD), bf16),
            pltpu.VMEM((128, 128), jnp.float32),
            pltpu.VMEM((128, 128), jnp.float32),
            pltpu.VMEM((ROWS, HD), jnp.float32),
            pltpu.VMEM((STEPS, QH * HD), jnp.float32),
            dma((2,)),
            dma((n // 2,)),
            dma((n // 2,)),
            dma((n,)),
            dma((n,)),
            dma((n,)),
            dma((2 * Z,)),
            dma((2 * Z,)),
            dma((2 * Z * X,)),
            dma((n,)),
            dma((n,)),
            dma((n,)),
        ],
        compiler_params=pltpu.CompilerParams(
            collective_id=0, has_side_effects=True, vmem_limit_bytes=56 * 1024 * 1024
        ),
    )(
        prompt_positions,
        page_owner.reshape(pages),
        page_fill,
        step_queries,
        prompt_queries,
        prompt_keys,
        prompt_values,
        step_keys,
        step_values,
        pool_keys.reshape(tokens, KVH * HD),
        pool_values.reshape(tokens, KVH * HD),
    )


def solution(mesh):
    rows = P(("group", "seq"), None)
    flat = P(("group", "seq"))
    cube = P(("group", "seq"), None, None)
    in_specs = (rows, rows, rows, flat, cube, cube, cube, cube, cube, rows, flat)
    return jax.shard_map(
        shards, mesh=mesh, in_specs=in_specs, out_specs=(rows, cube), check_vma=False
    )
```

```python
import functools
import jax
import jax.numpy as jnp
from jax import lax
from jax.experimental import pallas as pl
from jax.experimental.pallas import tpu as pltpu
from jax.sharding import PartitionSpec as P

QH = 32
KVH = 4
HD = 128
GROUP = QH // KVH
PAGE = 128
STEPS = 2
ROWS = STEPS * QH
HEAD_ROWS = STEPS * GROUP
MSG = ROWS + 16
SEQ_BLOCK = 16
NEG = -1e30
LOG2E = 1.4426950408889634
SCALE = HD ** (-0.5) * LOG2E
MESH = pl.DeviceIdType.MESH
NT = (((1,), (1,)), ((), ()))


def kernel(
    n,
    X,
    positions,
    page_owner,
    page_fill,
    step_q,
    pq,
    own_k,
    own_v,
    step_k,
    step_v,
    pool_k_hbm,
    pool_v_hbm,
    out,
    dec,
    qall,
    all_k,
    all_v,
    pool_k,
    pool_v,
    key_pos,
    tok_owner,
    psend,
    precv,
    stats,
    stats_in,
    own_q,
    own_dec,
    run_max,
    run_out,
    pool_sem,
    q_send,
    q_sib,
    q_recv,
    p_send,
    p_recv,
    up_send,
    down_send,
    x_send,
    sib_send,
    k_recv,
    v_recv,
):
    Z = n // (2 * X)
    half = n // 2
    me = lax.axis_index("seq")
    c = lax.rem(me, 2)
    x = lax.rem(me // 2, X)
    z = me // (2 * X)
    sib = me + 1 - 2 * c
    tok = own_k.shape[0]
    tokens = pool_k.shape[0]

    pool_copies = [
        pltpu.make_async_copy(pool_k_hbm, pool_k, pool_sem.at[0]),
        pltpu.make_async_copy(pool_v_hbm, pool_v, pool_sem.at[1]),
    ]
    barrier = pltpu.get_barrier_semaphore()

    def greet(i, carry):
        pl.semaphore_signal(
            barrier, inc=1, device_id={"seq": lax.rem(me + i, n)}, device_id_type=MESH
        )
        return carry

    lax.fori_loop(1, n, greet, 0)
    for copy in pool_copies:
        copy.start()
    all_k[me] = own_k[...]
    all_v[me] = own_v[...]
    wide_q = step_q[0].astype(jnp.float32)
    for j in range(QH):
        for i in range(STEPS):
            r = (j // GROUP) * HEAD_ROWS + i * GROUP + j % GROUP
            own_q[r : r + 1, :] = wide_q[i : i + 1, j * HD : (j + 1) * HD]
    qall[me, 0:ROWS, :] = own_q[...].astype(jnp.bfloat16)

    def row_position(i):
        return jnp.where(i < tok // 2, positions[0] + i, positions[tok // 2] + i - tok // 2)

    sub16 = lax.broadcasted_iota(jnp.int32, (16, 128), 0)
    lane_pos = row_position(lax.broadcasted_iota(jnp.int32, (16, 128), 1) % tok)
    coded = jnp.where(sub16 == 0, lane_pos // 128, lane_pos % 128)
    qall[me, ROWS:MSG, :] = coded.astype(jnp.float32).astype(jnp.bfloat16)
    stats[...] = jnp.full_like(stats, NEG)
    stats_in[...] = jnp.full_like(stats_in, NEG)
    pl.semaphore_wait(barrier, n - 1)

    def remote(buf, b, peer, ss, rs):
        return pltpu.make_async_remote_copy(
            src_ref=buf.at[b],
            dst_ref=buf.at[b],
            send_sem=ss,
            recv_sem=rs.at[b],
            device_id={"seq": peer},
            device_id_type=MESH,
        )

    def q_copy(j):
        return remote(qall, me, lax.rem(me + 2 * j, n), q_send.at[j], q_recv)

    def q_fwd(j):
        b = lax.rem(me + 2 * j, n)
        return remote(qall, b, sib, q_sib.at[j], q_recv)

    def loop(lo, hi, body):
        def step(i, carry):
            body(i)
            return carry

        lax.fori_loop(lo, hi, step, 0)

    loop(1, half, lambda j: q_copy(j).start())
    q_fwd(0).start()

    parts = ((0, all_k, k_recv), (1, all_v, v_recv))

    def to_up(b, zb, part):
        i, buf, rs = part
        return remote(buf, b, me + 2 * X, up_send.at[2 * zb + i], rs)

    def to_down(b, zb, part):
        i, buf, rs = part
        return remote(buf, b, me - 2 * X, down_send.at[2 * zb + i], rs)

    def to_x(b, zb, j, part):
        i, buf, rs = part
        peer = z * 2 * X + lax.rem(x + j, X) * 2 + c
        return remote(buf, b, peer, x_send.at[(zb * X + j) * 2 + i], rs)

    def to_sib(b, part):
        i, buf, rs = part
        return remote(buf, b, sib, sib_send.at[b // 2 * 2 + i], rs)

    def arrived(b, part):
        i, buf, rs = part
        remote(buf, b, sib, sib_send.at[i], rs).wait_recv()

    def column(zb):
        return zb * 2 * X + x * 2 + c

    def both(*conditions):
        bits = [jnp.where(one, 1, 0) for one in conditions]
        return functools.reduce(lambda p, q: p * q, bits) == 1

    def along_z(h, here):
        below, above = column(z - h), column(z + h)
        for part in parts:

            @pl.when(both(here, z >= h))
            def _():
                arrived(below, part)

            @pl.when(both(here, z >= h, z + 1 < Z))
            def _():
                to_up(below, z - h, part).start()

            @pl.when(both(here, z >= h))
            def _():
                for j in range(1, X):
                    to_x(below, z - h, j, part).start()
                to_sib(below, part).start()

            @pl.when(both(here, z + h < Z))
            def _():
                arrived(above, part)

            @pl.when(both(here, z + h < Z, z >= 1))
            def _():
                to_down(above, z + h, part).start()

            @pl.when(both(here, z + h < Z))
            def _():
                for j in range(1, X):
                    to_x(above, z + h, j, part).start()
                to_sib(above, part).start()

    def pass_on(zb, part):
        for j in range(1, X):
            b = zb * 2 * X + lax.rem(x + j, X) * 2 + c
            arrived(b, part)
            to_sib(b, part).start()

    def across_x(h, here):
        for part in parts:

            @pl.when(both(here, z >= h))
            def _():
                pass_on(z - h, part)

            if h > 0:

                @pl.when(both(here, z + h < Z))
                def _():
                    pass_on(z + h, part)

    def q_take(j):
        b = lax.rem(me + 2 * j, n)
        remote(qall, b, sib, q_sib.at[0], q_recv).wait_recv()
        q_fwd(j).start()

    loop(1, half, q_take)

    for part in parts:

        @pl.when(z + 1 < Z)
        def _():
            to_up(me, z, part).start()

        @pl.when(z >= 1)
        def _():
            to_down(me, z, part).start()

        for j in range(1, X):
            to_x(me, z, j, part).start()
        to_sib(me, part).start()

    def q_other(j):
        b = lax.rem(sib + 2 * j, n)
        remote(qall, b, sib, q_sib.at[0], q_recv).wait_recv()

    loop(0, half, q_other)

    lane = lax.broadcasted_iota(jnp.int32, (1, 2 * tok), 1)
    for i in range(half):
        pair = []
        for b in (2 * i, 2 * i + 1):
            coded = qall[b, ROWS:MSG, :].astype(jnp.float32)
            pair.append(coded[0:1] * 128.0 + coded[1:2])
        key_pos[:, i * 2 * tok : (i + 1) * 2 * tok] = jnp.where(lane < tok, pair[0], pair[1])

    page_lane = lax.broadcasted_iota(jnp.int32, (1, PAGE), 1)
    for p in range(tokens // PAGE):
        tok_owner[:, p * PAGE : (p + 1) * PAGE] = jnp.where(
            page_lane < page_fill[p], page_owner[p], -1
        )

    for copy in pool_copies:
        copy.wait()

    def fold(q, k, v, allowed, m, acc):
        s = lax.dot_general(q, k, NT, preferred_element_type=jnp.float32) * SCALE
        s = jnp.where(allowed, s, NEG)
        new = jnp.max(s, axis=1, keepdims=True)
        if m is not None:
            new = jnp.maximum(m, new)
        w = jnp.exp2(s - new).astype(jnp.bfloat16)
        wide = jnp.concatenate([v, jnp.ones_like(v)], axis=1)
        more = jnp.dot(w, wide, preferred_element_type=jnp.float32)
        return new, more if m is None else acc * jnp.exp2(m - new) + more

    chunk_tok = 512
    drows = SEQ_BLOCK * HEAD_ROWS
    row_seq = lax.broadcasted_iota(jnp.int32, (drows, 1), 0) // HEAD_ROWS
    lane16 = lax.broadcasted_iota(jnp.int32, (HEAD_ROWS, 128), 1)

    def decode_head(h):
        for k in range(1, min(Z, KVH)):
            along_z(k, h == k)
            across_x(k - 1, h == k)

        hrow = pl.multiple_of(h * HEAD_ROWS, HEAD_ROWS)
        hlane = pl.ds(pl.multiple_of(h * HD, HD), HD)

        def seq_block(sb):
            first = sb * SEQ_BLOCK
            q = qall[pl.ds(first, SEQ_BLOCK), pl.ds(hrow, HEAD_ROWS), :].reshape(drows, HD)

            def chunk(t, carry):
                at = pl.ds(t * chunk_tok, chunk_tok)
                allowed = tok_owner[:, at] == row_seq + first
                return fold(q, pool_k[at, hlane], pool_v[at, hlane], allowed, *carry)

            carry = (None, None)
            for t in range(tokens // chunk_tok):
                carry = chunk(t, carry)
            m, acc = carry
            l = acc[:, HD : HD + 1]
            o = (acc[:, :HD] / acc[:, HD:]).astype(jnp.bfloat16).reshape(SEQ_BLOCK, HEAD_ROWS, HD)
            psend[pl.ds(first, SEQ_BLOCK), pl.ds(hrow, HEAD_ROWS), :] = o
            lse = m + jnp.log2(l)
            seen = stats[pl.ds(hrow, HEAD_ROWS), :]
            for i in range(SEQ_BLOCK):
                seen = jnp.where(
                    lane16 == first + i, lse[i * HEAD_ROWS : (i + 1) * HEAD_ROWS], seen
                )
            stats[pl.ds(hrow, HEAD_ROWS), :] = seen

        loop(0, n // SEQ_BLOCK, seq_block)

    for h in range(KVH):
        decode_head(h)

    stats[...] = jnp.transpose(stats[...])
    def code(b):
        row = jnp.broadcast_to(stats[pl.ds(b, 1), :], (16, 128))
        hi = row.astype(jnp.bfloat16).astype(jnp.float32)
        mid = (row - hi).astype(jnp.bfloat16).astype(jnp.float32)
        low = row - hi - mid
        coded = jnp.where(sub16 == 0, hi, jnp.where(sub16 == 1, mid, low))
        psend[b, ROWS:MSG, :] = coded.astype(jnp.bfloat16)

    loop(0, n, code)

    def p_copy(j):
        b = lax.rem(me + j, n)
        return pltpu.make_async_remote_copy(
            src_ref=psend.at[b],
            dst_ref=precv.at[me],
            send_sem=p_send.at[j],
            recv_sem=p_recv.at[me],
            device_id={"seq": b},
            device_id_type=MESH,
        )

    loop(1, n, lambda j: p_copy(j).start())
    precv[me] = psend[me]

    for h in range(min(Z, KVH), Z):
        along_z(h, True)
        across_x(h - 1, True)

    def kv_other(side):
        def take(j):
            for part in parts:
                arrived(side * half + 2 * j + 1 - c, part)

        loop(0, half // 2, take)

    fan = 8
    pos_col = jnp.concatenate(
        [row_position(lax.broadcasted_iota(jnp.int32, (tok, 1), 0)).astype(jnp.float32)] * fan,
        axis=0,
    )
    chunk_keys = 512
    blocks = chunk_keys // tok

    side_keys = half * tok

    def prefill(u, side, last):
        h = u // (GROUP // fan)
        lanes = pl.ds(pl.multiple_of(h * HD, HD), HD)
        rows = pl.ds(u * fan * tok, fan * tok)
        q = jnp.concatenate(
            [pq[:, pl.ds(pl.multiple_of((u * fan + g) * HD, HD), HD)] for g in range(fan)],
            axis=0,
        )
        carry = (run_max[rows, 0:1], run_out[rows]) if last else (None, None)
        for t in range(side_keys // chunk_keys):
            at = pl.ds(side * half + t * blocks, blocks)
            key = all_k[at, :, lanes].reshape(chunk_keys, HD)
            value = all_v[at, :, lanes].reshape(chunk_keys, HD)
            first = pl.multiple_of(side * side_keys + t * chunk_keys, chunk_keys)
            pos = key_pos[:, pl.ds(first, chunk_keys)]
            carry = fold(q, key, value, pos <= pos_col, *carry)
        m, acc = carry
        if not last:
            run_max[rows] = jnp.broadcast_to(m, (fan * tok, HD))
            run_out[rows] = acc
            return
        o = (acc[:, :HD] / acc[:, HD:]).astype(jnp.bfloat16)
        for g in range(fan):
            out[:, pl.ds(pl.multiple_of((u * fan + g) * HD, HD), HD)] = o[g * tok : (g + 1) * tok]

    near = z // (Z // 2)
    kv_other(near)
    units = QH // fan
    for u in range(units):
        prefill(u, near, False)
        if u == 1:
            across_x(Z - 1, True)
    kv_other(1 - near)
    for u in range(units):
        prefill(u, 1 - near, True)

    def p_take(j):
        b = lax.rem(me + j, n)
        pltpu.make_async_remote_copy(
            src_ref=psend.at[b],
            dst_ref=precv.at[b],
            send_sem=p_send.at[0],
            recv_sem=p_recv.at[b],
            device_id={"seq": b},
            device_id_type=MESH,
        ).wait_recv()

    loop(1, n, p_take)

    def decode_stat(d):
        coded = precv[d, ROWS:MSG, :].astype(jnp.float32)
        stats_in[pl.ds(d, 1), :] = coded[0:1] + coded[1:2] + coded[2:3]

    loop(0, n, decode_stat)
    lse = jnp.transpose(stats_in[...])[0:ROWS]
    q = own_q[...]
    row_id = lax.broadcasted_iota(jnp.int32, (ROWS, 1), 0)
    row_step = (row_id // GROUP) % STEPS

    def per_row(wide, j):
        return jnp.concatenate(
            [
                jnp.broadcast_to(wide[j : j + 1, h * HD : (h + 1) * HD], (HEAD_ROWS, HD))
                for h in range(KVH)
            ],
            axis=0,
        )

    wide_k = step_k[0].astype(jnp.float32)
    wide_v = step_v[0].astype(jnp.float32)
    scores = []
    for j in range(STEPS):
        s = jnp.sum(q * per_row(wide_k, j), axis=1, keepdims=True) * SCALE
        scores.append(jnp.where(row_step >= j, s, NEG))
    top = jnp.max(lse, axis=1, keepdims=True)
    for s in scores:
        top = jnp.maximum(top, s)
    w = jnp.exp2(lse - top)
    denominator = jnp.sum(w, axis=1, keepdims=True)
    numerator = jnp.zeros((ROWS, HD), jnp.float32)
    for j in range(STEPS):
        e = jnp.exp2(scores[j] - top)
        denominator += e
        numerator += e * per_row(wide_v, j)
    dev = lax.broadcasted_iota(jnp.int32, (ROWS, 128), 1)

    def add(d, total):
        wd = jnp.sum(jnp.where(dev == d, w, 0.0), axis=1, keepdims=True)
        return total + wd * precv[d, 0:ROWS, :].astype(jnp.float32)

    numerator = lax.fori_loop(0, n, add, numerator, unroll=4)
    result = numerator / denominator
    for j in range(QH):
        for i in range(STEPS):
            r = (j // GROUP) * HEAD_ROWS + i * GROUP + j % GROUP
            own_dec[i : i + 1, j * HD : (j + 1) * HD] = result[r : r + 1]
    dec[0] = own_dec[...].astype(jnp.bfloat16)

    loop(1, half, lambda j: q_copy(j).wait_send())
    loop(0, half, lambda j: q_fwd(j).wait_send())
    loop(1, n, lambda j: p_copy(j).wait_send())
    for part in parts:
        for h in range(Z):

            @pl.when(both(z >= h, z + 1 < Z))
            def _():
                to_up(column(z - h), z - h, part).wait_send()

            @pl.when(both(z + h < Z, z >= 1))
            def _():
                to_down(column(z + h), z + h, part).wait_send()

        def left(zb):
            for j in range(1, X):
                to_x(column(zb), zb, j, part).wait_send()

        loop(0, Z, left)
        loop(0, half, lambda j: to_sib(2 * j + c, part).wait_send())


def shards(
    prompt_queries,
    prompt_keys,
    prompt_values,
    prompt_positions,
    step_queries,
    step_keys,
    step_values,
    pool_keys,
    pool_values,
    page_owner,
    page_fill,
):
    n = lax.axis_size("seq")
    X = max(1, round((n // 2) ** (1 / 3)))
    Z = n // (2 * X)
    tok = prompt_queries.shape[0]
    pages = pool_keys.shape[0]
    tokens = pages * PAGE
    vmem = pl.BlockSpec(memory_space=pltpu.VMEM)
    smem = pl.BlockSpec(memory_space=pltpu.SMEM)
    hbm = pl.BlockSpec(memory_space=pl.ANY)
    dma = pltpu.SemaphoreType.DMA
    bf16 = jnp.bfloat16
    return pl.pallas_call(
        functools.partial(kernel, n, X),
        out_shape=(
            jax.ShapeDtypeStruct((tok, QH * HD), bf16),
            jax.ShapeDtypeStruct((1, STEPS, QH * HD), bf16),
        ),
        in_specs=[smem] * 3 + [vmem] * 6 + [hbm] * 2,
        out_specs=(vmem, vmem),
        scratch_shapes=[
            pltpu.VMEM((n, MSG, HD), bf16),
            pltpu.VMEM((n, tok, KVH * HD), bf16),
            pltpu.VMEM((n, tok, KVH * HD), bf16),
            pltpu.VMEM((tokens, KVH * HD), bf16),
            pltpu.VMEM((tokens, KVH * HD), bf16),
            pltpu.VMEM((1, n * tok), jnp.float32),
            pltpu.VMEM((1, tokens), jnp.int32),
            pltpu.VMEM((n, MSG, HD), bf16),
            pltpu.VMEM((n, MSG, HD), bf16),
            pltpu.VMEM((128, 128), jnp.float32),
            pltpu.VMEM((128, 128), jnp.float32),
            pltpu.VMEM((ROWS, HD), jnp.float32),
            pltpu.VMEM((STEPS, QH * HD), jnp.float32),
            pltpu.VMEM((QH * tok, HD), jnp.float32),
            pltpu.VMEM((QH * tok, 2 * HD), jnp.float32),
            dma((2,)),
            dma((n // 2,)),
            dma((n // 2,)),
            dma((n,)),
            dma((n,)),
            dma((n,)),
            dma((2 * Z,)),
            dma((2 * Z,)),
            dma((2 * Z * X,)),
            dma((n,)),
            dma((n,)),
            dma((n,)),
        ],
        compiler_params=pltpu.CompilerParams(
            collective_id=0, has_side_effects=True, vmem_limit_bytes=56 * 1024 * 1024
        ),
    )(
        prompt_positions,
        page_owner.reshape(pages),
        page_fill,
        step_queries,
        prompt_queries,
        prompt_keys,
        prompt_values,
        step_keys,
        step_values,
        pool_keys.reshape(tokens, KVH * HD),
        pool_values.reshape(tokens, KVH * HD),
    )


def solution(mesh):
    rows = P(("group", "seq"), None)
    flat = P(("group", "seq"))
    cube = P(("group", "seq"), None, None)
    in_specs = (rows, rows, rows, flat, cube, cube, cube, cube, cube, rows, flat)
    return jax.shard_map(
        shards, mesh=mesh, in_specs=in_specs, out_specs=(rows, cube), check_vma=False
    )
```
